32 devices in a mesh: gx: 4 (over z), gy: 4 (over y, x), gz: 2 (over core).
Axes of the slice: x: 2, y: 2, z: 4, core: 2. Of those that a mesh axis runs over, the one named last changes fastest.
Arguments:
- distribution: bfloat16 [8, 32, 16, 12, 512], P('gx', 'gy', 'gz'), may hold values from 0.019897461 to 1
- block_ids: int32 [8, 32, 16, 12], P('gx', 'gy', 'gz'), may hold values from 0 to 215, as said below
- cell_counts: int32 [8, 32, 16], P('gx', 'gy', 'gz'), may hold values from 6 to 12
- owner: int32 [8, 32, 16], P('gx', 'gy', 'gz'), may hold values from 0 to 7, as said below
- restitution: bfloat16 [8, 32, 16], P('gx', 'gy', 'gz'), may hold values from 0.5 to 0.94921875
Outputs:
- moved_distribution: bfloat16 [4, 1024, 12, 512], P('gy', ('gx', 'gz'))
- moved_ids: int32 [4, 1024, 12], P('gy', ('gx', 'gz'))
- moved_counts: int32 [4, 1024], P('gy', ('gx', 'gz'))
The draws below stay inside these ranges and needn't reach their ends.
Inputs may be any that keep to these rules, and one draw needn't show every extreme that they name: `block_ids`: the 12 numbers of one cell are distinct block numbers. `owner`: owner g means the device of the cell's gy row with gx index g // 2 and gz index g % 2. Each device sends exactly 16 of its cells to each of the 8 devices of its gy row (itself included), and each device owns exactly 128 cells afterwards.
All inputs are finite; a program needn't handle non-finite values.
Results may differ from the reference program's by a relative error of at most 0.001.
The reference program's roundings to bfloat16 on the way (of `read` and `relaxed`) count: a program that leaves them out, or rounds other values in their place, can miss the bound.
Values may be sent and summed in bfloat16 or wider, within the bound.
A program may use at most 64 MiB of HBM per device.

```python
import math
import jax
import jax.numpy as jnp
import numpy as np
from jax import lax

NV1 = 48
BLK = 8
MAXB = 12
CX = 2
CY = 8
CZ = 8
VB = 512
CELLS = 128
NX = 8
NY = 32
NZ = 16
GROUP = 8
CAPS = 16
N_GX = 4
N_GY = 4
N_GZ = 2


def neighbour_table():
    entries = []
    for first in (-1, 0, 1):
        for second in (-1, 0, 1):
            for third in (-1, 0, 1):
                if first != 0 or second != 0 or third != 0:
                    entries.append((first, second, third))
    return np.array(entries, dtype=np.int32)


def draw_block_ids(key, part):
    blocks_edge = NV1 // BLK
    total_cells = NX * NY * NZ
    first_key, second_key = jax.random.split(jax.random.fold_in(key, 11))
    centers = jax.random.randint(first_key, (total_cells, 3), 1, blocks_edge - 1)
    centers = centers.at[0].set(jnp.ones((3,), jnp.int32))
    centers = centers.at[total_cells - 1].set(jnp.full((3,), blocks_edge - 2, jnp.int32))
    scores = jax.random.randint(second_key, (total_cells, 26), 0, 1 << 20) * 32 + jnp.arange(26, dtype=jnp.int32)
    scores = scores.at[0, 0].set(-1)
    scores = scores.at[total_cells - 1, 25].set(-1)
    ordering = jnp.argsort(scores, axis=-1)[..., :MAXB - 1]
    offset_table = jnp.asarray(neighbour_table())
    chosen = offset_table[ordering]
    coords = jnp.concatenate([centers[..., None, :], centers[..., None, :] + chosen], axis=-2)
    ids = (coords[..., 0] * blocks_edge + coords[..., 1]) * blocks_edge + coords[..., 2]
    return ids.reshape(NX, NY, NZ, MAXB).astype(jnp.int32)


def draw_cell_counts(key, part):
    first_key, second_key = jax.random.split(jax.random.fold_in(key, 23))
    drawn = jax.random.randint(first_key, (NX * NY * NZ,), MAXB // 2, MAXB + 1)
    chosen_cell = jax.random.randint(second_key, (), 0, NX * NY * NZ)
    drawn = drawn.at[chosen_cell].set(MAXB)
    return drawn.reshape(NX, NY, NZ).astype(jnp.int32)


def draw_owner(key, part):
    first_key, second_key = jax.random.split(jax.random.fold_in(key, 37))
    rotation = jax.vmap(lambda one_key: jax.random.permutation(one_key, GROUP))(jax.random.split(first_key, N_GY))
    inverse = jnp.argsort(rotation, axis=1)
    placement = jax.vmap(lambda one_key: jax.random.permutation(one_key, CELLS))(jax.random.split(second_key, N_GY * GROUP))
    placement = placement.reshape(N_GY, GROUP, CELLS)
    step_count = placement // CAPS
    shifted = (rotation[:, :, None] + step_count) % GROUP
    destination_holder = jnp.take_along_axis(inverse[:, None, :], shifted.reshape(N_GY, 1, GROUP * CELLS), axis=2)
    destination_holder = destination_holder.reshape(N_GY, N_GX, N_GZ, CX, CY, CZ)
    destination_holder = destination_holder.transpose((1, 3, 0, 4, 2, 5)).reshape(NX, NY, NZ)
    return destination_holder.astype(jnp.int32)


def shard_levels(own_key, shape, cuts, smallest, top_value):
    def one(position, parts):
        draws = jax.random.uniform(jax.random.fold_in(jax.random.fold_in(own_key, 6), position), (parts,), jnp.float32, smallest / len(cuts), top_value / len(cuts))
        return jnp.repeat(jnp.exp(draws), shape[position] // parts).reshape((-1,) + (1,) * (len(shape) - position - 1))

    level = one(*cuts[0])
    for cut in cuts[1:]:
        level = level * one(*cut)
    return level


def setup_inputs(seed: int = 0) -> dict:
    keys = jax.random.split(jax.random.key(seed), 6)
    return {
        "distribution": jnp.clip(jnp.exp(math.log(1.0) - 3.9171631 * jax.random.uniform(keys[0], (NX, NY, NZ, MAXB, VB), jnp.float32) ** shard_levels(keys[0], (NX, NY, NZ, MAXB, VB), ((0, 4), (1, 4), (2, 2)), -0.2, 0.2)), 0.019897461, 1.0).astype(jnp.bfloat16),
        "block_ids": draw_block_ids(jax.random.fold_in(keys[5], 71), 0),
        "cell_counts": draw_cell_counts(jax.random.fold_in(keys[5], 71), 0),
        "owner": draw_owner(jax.random.fold_in(keys[5], 71), 0),
        "restitution": jnp.clip(0.5 + 0.44921875 * jax.random.uniform(keys[4], (NX, NY, NZ), jnp.float32) ** shard_levels(keys[4], (NX, NY, NZ), ((0, 4), (1, 4), (2, 2)), -0.2, 0.2), 0.5, 0.94921875).astype(jnp.bfloat16),
    }


STEP_COEFF = 0.6
IMPACT_KIND = 0.02

def inner_offsets():
    velocity_index = jnp.arange(BLK ** 3, dtype=jnp.int32)
    coords = jnp.stack([velocity_index // (BLK * BLK), velocity_index // BLK % BLK, velocity_index % BLK])
    return coords.astype(jnp.float32) - (BLK - 1) / 2.0

def block_centers(ids):
    blocks_edge = NV1 // BLK
    coords = jnp.stack([ids // (blocks_edge * blocks_edge), ids // blocks_edge % blocks_edge, ids % blocks_edge])
    return coords.astype(jnp.float32) * BLK + (BLK - 1) / 2.0 - (NV1 - 1) / 2.0

def neighbor_values(own_ids, other_ids, other_values):
    matches = ((own_ids[..., :, None] == other_ids[..., None, :]) & (own_ids[..., :, None] >= 0)).astype(jnp.int32)
    chosen = jnp.argmax(matches, axis=-1).astype(jnp.int32)
    found_any = lax.optimization_barrier(jnp.max(matches, axis=-1)).astype(jnp.float32)
    picked = jnp.take_along_axis(other_values, chosen[..., None], axis=-2).astype(jnp.float32)
    return picked * found_any[..., None]

def transport(values, raw_ids, own_ids, live_mask, neighbours):
    inner_offset = inner_offsets()
    centers = block_centers(raw_ids)
    center_value = values.astype(jnp.float32)
    flux_sum = jnp.zeros(center_value.shape, jnp.float32)
    lam = STEP_COEFF / (NV1 - 1)
    for direction in range(3):
        lower_vals, lower_ids, upper_vals, upper_ids = neighbours[direction]
        velocity = centers[direction][..., None] + inner_offset[direction]
        from_lower = neighbor_values(own_ids, lower_ids, lower_vals)
        from_upper = neighbor_values(own_ids, upper_ids, upper_vals)
        flux_sum = flux_sum + jnp.maximum(velocity, 0.0) * (center_value - from_lower) + jnp.minimum(velocity, 0.0) * (from_upper - center_value)
    return ((center_value - lam * flux_sum) * live_mask[..., None]).astype(jnp.bfloat16)

def relax(read, raw_ids, live_mask, coefficient):
    inner_offset = inner_offsets()
    centers = block_centers(raw_ids)
    tile_span = inner_offset.shape[1]
    squares = lax.optimization_barrier(jnp.sum(inner_offset * inner_offset, axis=0))
    weights_table = jnp.concatenate([jnp.ones((1, tile_span), jnp.float32), inner_offset, squares[None]], axis=0).T.astype(jnp.bfloat16)
    leading = read.shape[:-1]
    block_sums = jnp.dot(read.reshape(-1, tile_span), weights_table, preferred_element_type=jnp.float32).reshape(leading + (5,))
    block_mass = block_sums[..., 0]
    particle_count_field = lax.optimization_barrier(jnp.sum(block_mass, axis=-1))
    momentum = [lax.optimization_barrier(jnp.sum(block_mass * centers[k] + block_sums[..., 1 + k], axis=-1)) for k in range(3)]
    center_sq = centers[0] * centers[0] + centers[1] * centers[1] + centers[2] * centers[2]
    cross = centers[0] * block_sums[..., 1] + centers[1] * block_sums[..., 2] + centers[2] * block_sums[..., 3]
    motion_work_sum = lax.optimization_barrier(jnp.sum(block_mass * center_sq + 2.0 * cross + block_sums[..., 4], axis=-1))
    average_drift = [momentum[k] / particle_count_field for k in range(3)]
    thermal_spread = (motion_work_sum / particle_count_field - (average_drift[0] * average_drift[0] + average_drift[1] * average_drift[1] + average_drift[2] * average_drift[2])) / 3.0
    return_parcels_home = coefficient.astype(jnp.float32)
    destination_holder = thermal_spread * (1.0 + return_parcels_home) * (1.0 + return_parcels_home) / 4.0
    equilibration_frequency = 1.0 - jnp.exp(-IMPACT_KIND * (particle_count_field / tile_span) * jnp.sqrt(thermal_spread))
    distance = jnp.zeros(read.shape, jnp.float32)
    for k in range(3):
        offset_k = centers[k][..., None] + inner_offset[k] - average_drift[k][..., None, None]
        distance = distance + offset_k * offset_k
    scale = particle_count_field / (2.0 * math.pi * destination_holder) ** 1.5
    maxwellian = scale[..., None, None] * jnp.exp(-distance / (2.0 * destination_holder[..., None, None]))
    stream_vals = read.astype(jnp.float32)
    relaxed = (stream_vals + equilibration_frequency[..., None, None] * (maxwellian - stream_vals)) * live_mask[..., None]
    return relaxed.astype(jnp.bfloat16)

def to_groups(array):
    trailing = array.shape[3:]
    shaped = array.reshape((N_GX, CX, N_GY, CY, N_GZ, CZ) + trailing)
    shaped = shaped.transpose((2, 0, 4, 1, 3, 5) + tuple(range(6, 6 + len(trailing))))
    return shaped.reshape((N_GY, N_GX * N_GZ * CX * CY * CZ) + trailing)

def reference(distribution, block_ids, cell_counts, owner, restitution):
    slot_index = jnp.arange(MAXB, dtype=jnp.int32)
    live = slot_index < cell_counts[..., None]
    listed = jnp.where(live, block_ids, -1)

    def plane_step(plane_index):
        prev_plane = (plane_index + NX - 1) % NX
        next_plane = (plane_index + 1) % NX
        values = distribution[plane_index]
        own_ids = listed[plane_index]
        neighbours = [(distribution[prev_plane], listed[prev_plane], distribution[next_plane], listed[next_plane]), (jnp.roll(values, 1, 0), jnp.roll(own_ids, 1, 0), jnp.roll(values, -1, 0), jnp.roll(own_ids, -1, 0)), (jnp.roll(values, 1, 1), jnp.roll(own_ids, 1, 1), jnp.roll(values, -1, 1), jnp.roll(own_ids, -1, 1))]
        live_mask = live[plane_index].astype(jnp.float32)
        read = transport(values, block_ids[plane_index], own_ids, live_mask, neighbours)
        return relax(read, block_ids[plane_index], live_mask, restitution[plane_index])
    relaxed_cells = lax.map(plane_step, jnp.arange(NX, dtype=jnp.int32))
    owner_rows = to_groups(owner)
    ordering = jnp.argsort(owner_rows, axis=1, stable=True).astype(jnp.int32)
    moved_distribution = jnp.take_along_axis(to_groups(relaxed_cells), ordering[..., None, None], axis=1)
    moved_ids = jnp.take_along_axis(to_groups(block_ids), ordering[..., None], axis=1)
    moved_counts = jnp.take_along_axis(to_groups(cell_counts), ordering, axis=1)
    return (moved_distribution, moved_ids, moved_counts)
```

```python
import functools
import math

import jax
import jax.numpy as jnp
from jax import lax
from jax.experimental import pallas as pl
from jax.experimental.pallas import tpu as pltpu
from jax.sharding import PartitionSpec as P

NV1 = 48
BLK = 8
EDGE = NV1 // BLK
STEP_COEFF = 0.6
IMPACT_KIND = 0.02
ZPAD = 16


def weights():
    j = jnp.arange(BLK**3, dtype=jnp.int32)
    w = [c.astype(jnp.float32) - (BLK - 1) / 2.0 for c in (j // (BLK * BLK), j // BLK % BLK, j % BLK)]
    cols = [jnp.ones_like(w[0]), *w, w[0] * w[0] + w[1] * w[1] + w[2] * w[2]]
    return jnp.concatenate([jnp.broadcast_to(c[:, None], (BLK**3, 128)) for c in cols], axis=1).astype(jnp.bfloat16)


def column(slots, sz, ext_x, ext_y, own, zrows, xkeys, ykeys, zkeys, ids, coef, w_ref):
    rows = slots * sz
    shape = (rows, 128)
    listed = jnp.broadcast_to(ids, shape)
    live = listed >= 0
    z = lax.broadcasted_iota(jnp.int32, shape, 0) % sz
    bx = (listed * 1821) >> 16
    rem = listed - bx * (EDGE * EDGE)
    by = (rem * 10923) >> 16
    bz = rem - by * EDGE
    half = EDGE // 2

    def match(key, other):
        key = jnp.where(live, key, -5)[:, :1]
        return jnp.where(key == other, 1.0, 0.0).astype(jnp.bfloat16)

    mx = match(listed + 256 * z + jnp.where(bx >= half, 0, 4096), xkeys)
    my = match(listed + 256 * z + jnp.where(by >= half, 0, 4096), ykeys)
    mz = match(listed + 256 * jnp.where(bz >= half, z, z + 2), zkeys)
    dot = functools.partial(jnp.dot, preferred_element_type=jnp.float32)
    gx = dot(mx, jnp.concatenate(ext_x, axis=0))
    gy = dot(my, jnp.concatenate(ext_y, axis=0))
    gz = dot(mz, jnp.concatenate([own, zrows], axis=0))

    offset = (BLK - 1) / 2.0 - (NV1 - 1) / 2.0
    c = [b.astype(jnp.float32) * BLK + offset for b in (bx, by, bz)]
    lane = lax.broadcasted_iota(jnp.int32, (1, 128), 1)
    mid = (BLK - 1) / 2.0
    wx = [(lane // 64 + 2 * t).astype(jnp.float32) - mid for t in range(4)]
    wy = (lane // BLK % BLK).astype(jnp.float32) - mid
    wz = (lane % BLK).astype(jnp.float32) - mid
    vy, vz = jnp.abs(c[1] + wy), jnp.abs(c[2] + wz)
    lam = STEP_COEFF / (NV1 - 1)
    reads = []
    for t in range(4):
        cut = slice(128 * t, 128 * (t + 1))
        f = own[:, cut].astype(jnp.float32)
        flux = jnp.abs(c[0] + wx[t]) * (f - gx[:, cut]) + vy * (f - gy[:, cut]) + vz * (f - gz[:, cut])
        reads.append(jnp.where(live, f - lam * flux, 0.0).astype(jnp.bfloat16))
    sums = dot(reads[0], w_ref[0:128, :])
    for t in range(1, 4):
        sums = sums + dot(reads[t], w_ref[128 * t : 128 * (t + 1), :])
    s = [sums[:, 128 * k : 128 * (k + 1)] for k in range(5)]

    def per_cell(a):
        return jnp.sum(a.reshape(slots, sz, 128), axis=0)

    mass = per_cell(s[0])
    momentum = [per_cell(s[0] * c[k] + s[1 + k]) for k in range(3)]
    sq = c[0] * c[0] + c[1] * c[1] + c[2] * c[2]
    cross = c[0] * s[1] + c[1] * s[2] + c[2] * s[3]
    energy = per_cell(s[0] * sq + 2.0 * cross + s[4])
    u = [m / mass for m in momentum]
    temperature = (energy / mass - (u[0] * u[0] + u[1] * u[1] + u[2] * u[2])) / 3.0
    target = temperature * (1.0 + coef) * (1.0 + coef) / 4.0
    rate = 1.0 - jnp.exp(-IMPACT_KIND * (mass / BLK**3) * jnp.sqrt(temperature))
    area = 2.0 * math.pi * target
    scale = mass / (area * jnp.sqrt(area))
    inv = -0.5 / target

    cube = (slots, sz, 128)
    a = [c[k].reshape(cube) - u[k][None] for k in range(3)]
    oy, oz = a[1] + wy[None], a[2] + wz[None]
    q = oy * oy + oz * oz
    live3 = listed.reshape(cube) >= 0
    outs = []
    for t in range(4):
        ox = a[0] + wx[t][None]
        maxwellian = scale[None] * jnp.exp((ox * ox + q) * inv[None])
        r = reads[t].astype(jnp.float32).reshape(cube)
        outs.append(jnp.where(live3, r + rate[None] * (maxwellian - r), 0.0))
    return outs


def compute_kernel(sizes, ext, zh, xk, yk, zk, ids, coef, w_ref, pos, out, pay):
    cx, cy, sz, slots, groups, cap = sizes

    def body(n, carry):
        x, y = n // cy, n % cy
        outs = column(
            slots, sz,
            [ext[x, y + 1], ext[x + 2, y + 1]],
            [ext[x + 1, y], ext[x + 1, y + 2]],
            ext[x + 1, y + 1], zh[n], xk[n], yk[n], zk[n], ids[n], coef[n], w_ref,
        )
        for t in range(4):
            pay[:, pl.ds(pl.multiple_of(n * sz, sz), sz), 128 * t : 128 * (t + 1)] = outs[t]
        return carry

    lax.fori_loop(0, cx * cy, body, 0)
    cells = cx * cy * sz
    perm = jnp.where(lax.broadcasted_iota(jnp.int32, (cells, cells), 0) == pos[...], 1.0, 0.0).astype(jnp.bfloat16)

    def send(s, carry):
        rows = jnp.dot(perm, pay[s].astype(jnp.bfloat16), preferred_element_type=jnp.float32)
        for g in range(groups):
            out[g, s] = rows[g * cap : (g + 1) * cap].astype(jnp.bfloat16)
        return carry

    lax.fori_loop(0, slots, send, 0)


def shifted(value, axis, step):
    peers = lax.axis_size(axis)
    return lax.ppermute(value, axis, [(i, (i + step) % peers) for i in range(peers)])


def on_device(distribution, block_ids, cell_counts, owner, restitution):
    cx, cy, sz, slots, vb = distribution.shape
    cells, rows = cx * cy * sz, slots * sz
    groups = lax.axis_size("gx") * lax.axis_size("gz")
    cap = cells // groups
    live = jnp.arange(slots, dtype=jnp.int32) < cell_counts[..., None]
    listed = jnp.where(live, block_ids, -1).transpose(0, 1, 3, 2)
    f = distribution.transpose(0, 1, 3, 2, 4)

    xlo, xhi = shifted(f[-1:], "gx", 1), shifted(f[:1], "gx", -1)
    ylo, yhi = shifted(f[:, -1:], "gy", 1), shifted(f[:, :1], "gy", -1)
    zlo, zhi = shifted(f[:, :, :, -1], "gz", 1), shifted(f[:, :, :, 0], "gz", -1)
    ixlo, ixhi = shifted(listed[-1:], "gx", 1), shifted(listed[:1], "gx", -1)
    iylo, iyhi = shifted(listed[:, -1:], "gy", 1), shifted(listed[:, :1], "gy", -1)
    izlo, izhi = shifted(listed[..., -1], "gz", 1), shifted(listed[..., 0], "gz", -1)

    middle = jnp.concatenate([ylo, f, yhi], axis=1)
    wide = ((0, 0), (1, 1), (0, 0), (0, 0), (0, 0))
    ext = jnp.concatenate([jnp.pad(xlo, wide), middle, jnp.pad(xhi, wide)], axis=0)
    ext = ext.reshape(cx + 2, cy + 2, rows, vb)
    pad = ((0, 0), (0, 0), (0, ZPAD - slots), (0, 0))
    zh = jnp.concatenate([jnp.pad(zlo, pad), jnp.pad(zhi, pad)], axis=2).reshape(cx * cy, 2 * ZPAD, vb)

    keyed = lambda ids: (ids + 256 * jnp.arange(sz, dtype=jnp.int32)).reshape(ids.shape[0], ids.shape[1], rows)
    xk = keyed(jnp.concatenate([ixlo, listed, ixhi], axis=0))
    xk = jnp.concatenate([xk[:-2], xk[2:] + 4096], axis=-1).reshape(cx * cy, 1, 2 * rows)
    yk = keyed(jnp.concatenate([iylo, listed, iyhi], axis=1))
    yk = jnp.concatenate([yk[:, :-2], yk[:, 2:] + 4096], axis=-1).reshape(cx * cy, 1, 2 * rows)
    none = ((0, 0), (0, 0), (0, ZPAD - slots))
    zk = jnp.concatenate(
        [
            keyed(listed) + 256,
            jnp.pad(izlo, none, constant_values=-9),
            jnp.pad(izhi + 256 * (sz + 1), none, constant_values=-9),
        ],
        axis=-1,
    ).reshape(cx * cy, 1, rows + 2 * ZPAD)
    ids = listed.reshape(cx * cy, rows, 1)
    coef = jnp.broadcast_to(restitution.astype(jnp.float32).reshape(cx * cy, sz, 1), (cx * cy, sz, 128))

    owners = owner.reshape(cells)
    order = jnp.arange(cells, dtype=jnp.int32)
    same = (owners[:, None] == owners[None, :]) & (order[:, None] < order[None, :])
    pos = owners * cap + jnp.sum(same.astype(jnp.int32), axis=0)

    meta = jnp.concatenate([block_ids.reshape(cells, slots), cell_counts.reshape(cells, 1)], axis=1)
    onehot = (order[:, None] == pos[None, :]).astype(jnp.bfloat16)
    meta = jnp.dot(onehot, meta.astype(jnp.bfloat16), preferred_element_type=jnp.float32).astype(jnp.bfloat16)
    meta = lax.all_to_all(meta, ("gx", "gz"), split_axis=0, concat_axis=0, tiled=True).astype(jnp.int32)

    sizes = (cx, cy, sz, slots, groups, cap)
    outgoing = pl.pallas_call(
        functools.partial(compute_kernel, sizes),
        out_shape=jax.ShapeDtypeStruct((groups, slots, cap, vb), jnp.bfloat16),
        in_specs=[pl.BlockSpec(memory_space=pltpu.VMEM)] * 9,
        out_specs=pl.BlockSpec(memory_space=pltpu.VMEM),
        scratch_shapes=[pltpu.VMEM((slots, cells, vb), jnp.float32)],
        compiler_params=pltpu.CompilerParams(vmem_limit_bytes=40 << 20),
        name="transport_relax",
    )(ext, zh, xk, yk, zk, ids, coef, weights(), pos.reshape(1, cells))
    received = lax.all_to_all(outgoing, ("gx", "gz"), split_axis=0, concat_axis=0, tiled=True)
    moved = received.transpose(0, 2, 1, 3).reshape(1, cells, slots, vb)
    return moved, meta[:, :slots].reshape(1, cells, slots), meta[:, slots].reshape(1, cells)


def solution(mesh):
    placed = (
        P("gx", "gy", "gz", None, None),
        P("gx", "gy", "gz", None),
        P("gx", "gy", "gz"),
        P("gx", "gy", "gz"),
        P("gx", "gy", "gz"),
    )
    return jax.shard_map(
        on_device,
        mesh=mesh,
        in_specs=placed,
        out_specs=(
            P("gy", ("gx", "gz"), None, None),
            P("gy", ("gx", "gz"), None),
            P("gy", ("gx", "gz")),
        ),
        check_vma=False,
    )
```

```python
import functools
import math

import jax
import jax.numpy as jnp
from jax import lax
from jax.experimental import pallas as pl
from jax.experimental.pallas import tpu as pltpu
from jax.sharding import PartitionSpec as P

NV1 = 48
BLK = 8
EDGE = NV1 // BLK
STEP_COEFF = 0.6
IMPACT_KIND = 0.02
ZPAD = 16
XPARTS = 4
PARTS = 4


def weights():
    j = jnp.arange(BLK**3, dtype=jnp.int32)
    w = [c.astype(jnp.float32) - (BLK - 1) / 2.0 for c in (j // (BLK * BLK), j // BLK % BLK, j % BLK)]
    cols = [jnp.ones_like(w[0]), *w, w[0] * w[0] + w[1] * w[1] + w[2] * w[2]]
    return jnp.concatenate([jnp.broadcast_to(c[:, None], (BLK**3, 128)) for c in cols], axis=1).astype(jnp.bfloat16)


def column(slots, sz, ext_x, ext_y, own, zrows, xkeys, ykeys, own_keys, zkeys, ids, coef, w_ref):
    rows = slots * sz
    shape = (rows, 128)
    listed = jnp.broadcast_to(ids, shape)
    live = listed >= 0
    z = lax.broadcasted_iota(jnp.int32, shape, 0) % sz
    bx = (listed * 1821) >> 16
    rem = listed - bx * (EDGE * EDGE)
    by = (rem * 10923) >> 16
    bz = rem - by * EDGE
    half = EDGE // 2

    dot = functools.partial(jnp.dot, preferred_element_type=jnp.float32)

    def pick(key, others, values):
        key = jnp.where(live, key, -5)[:, :1]
        total = None
        for other, value in zip(others, values):
            hit = jnp.where(key == other[:, : value.shape[0]], 1.0, 0.0).astype(jnp.bfloat16)
            got = dot(hit, value)
            total = got if total is None else total + got
        return total

    here = listed + 256 * z
    gx = pick(here + jnp.where(bx >= half, 0, 4096), (xkeys[0], xkeys[1] + 4096), ext_x)
    gy = pick(here + jnp.where(by >= half, 0, 4096), (ykeys[0], ykeys[1] + 4096), ext_y)
    zkey = listed + 256 * jnp.where(bz >= half, z, z + 2)
    gz = pick(zkey, (own_keys + 256, *zkeys), (own, *zrows))

    offset = (BLK - 1) / 2.0 - (NV1 - 1) / 2.0
    c = [b.astype(jnp.float32) * BLK + offset for b in (bx, by, bz)]
    lane = lax.broadcasted_iota(jnp.int32, (1, 128), 1)
    mid = (BLK - 1) / 2.0
    wx = [(lane // 64 + 2 * t).astype(jnp.float32) - mid for t in range(4)]
    wy = (lane // BLK % BLK).astype(jnp.float32) - mid
    wz = (lane % BLK).astype(jnp.float32) - mid
    vy, vz = jnp.abs(c[1] + wy), jnp.abs(c[2] + wz)
    lam = STEP_COEFF / (NV1 - 1)
    reads = []
    for t in range(4):
        cut = slice(128 * t, 128 * (t + 1))
        f = own[:, cut].astype(jnp.float32)
        flux = jnp.abs(c[0] + wx[t]) * (f - gx[:, cut]) + vy * (f - gy[:, cut]) + vz * (f - gz[:, cut])
        reads.append(jnp.where(live, f - lam * flux, 0.0).astype(jnp.bfloat16))
    sums = dot(reads[0], w_ref[0:128, :])
    for t in range(1, 4):
        sums = sums + dot(reads[t], w_ref[128 * t : 128 * (t + 1), :])
    s = [sums[:, 128 * k : 128 * (k + 1)] for k in range(5)]

    def per_cell(a):
        return jnp.sum(a.reshape(slots, sz, 128), axis=0)

    mass = per_cell(s[0])
    momentum = [per_cell(s[0] * c[k] + s[1 + k]) for k in range(3)]
    sq = c[0] * c[0] + c[1] * c[1] + c[2] * c[2]
    cross = c[0] * s[1] + c[1] * s[2] + c[2] * s[3]
    energy = per_cell(s[0] * sq + 2.0 * cross + s[4])
    u = [m / mass for m in momentum]
    temperature = (energy / mass - (u[0] * u[0] + u[1] * u[1] + u[2] * u[2])) / 3.0
    target = temperature * (1.0 + coef) * (1.0 + coef) / 4.0
    rate = 1.0 - jnp.exp(-IMPACT_KIND * (mass / BLK**3) * jnp.sqrt(temperature))
    area = 2.0 * math.pi * target
    scale = mass / (area * jnp.sqrt(area))
    inv = -0.5 / target

    cube = (slots, sz, 128)
    a = [c[k].reshape(cube) - u[k][None] for k in range(3)]
    oy, oz = a[1] + wy[None], a[2] + wz[None]
    q = oy * oy + oz * oz
    live3 = listed.reshape(cube) >= 0
    outs = []
    for t in range(4):
        ox = a[0] + wx[t][None]
        maxwellian = scale[None] * jnp.exp((ox * ox + q) * inv[None])
        r = reads[t].astype(jnp.float32).reshape(cube)
        outs.append(jnp.where(live3, r + rate[None] * (maxwellian - r), 0.0))
    return outs


MESH = pl.DeviceIdType.MESH


def whole_kernel(
    sizes, f, zlast, zfirst, krow, klast, kfirst, meta, ids, coef, w_ref, pos,
    out, meta_out,
    ext, zlo, zhi, kext, kzlo, kzhi, pay, sendb, x_sem, face_sem, local_sem, move_sem, meta_sem,
):
    cx, cy, sz, slots, groups, cap, xparts, parts = sizes
    gx, gy, gz = (lax.axis_index(a) for a in ("gx", "gy", "gz"))
    nx, ny, nz = (lax.axis_size(a) for a in ("gx", "gy", "gz"))
    me = gx * nz + gz
    up_x, down_x = ((gx + 1) % nx, gy, gz), ((gx + nx - 1) % nx, gy, gz)
    up_y, down_y = (gx, (gy + 1) % ny, gz), (gx, (gy + ny - 1) % ny, gz)
    up_z, down_z = (gx, gy, (gz + 1) % nz), (gx, gy, (gz + nz - 1) % nz)

    def peer(d):
        other = (me + d) % groups
        return other // nz, gy, other % nz

    barrier = pltpu.get_barrier_semaphore()
    pl.semaphore_signal(barrier, inc=1, device_id=up_y, device_id_type=MESH)
    pl.semaphore_signal(barrier, inc=1, device_id=down_y, device_id_type=MESH)

    def greet(d, carry):
        pl.semaphore_signal(barrier, inc=1, device_id=peer(d), device_id_type=MESH)
        return carry

    lax.fori_loop(1, groups, greet, 0)

    inner = pltpu.make_async_copy(f, ext.at[pl.ds(1, cx), pl.ds(1, cy)], local_sem.at[0])
    inner.start()
    inner_keys = pltpu.make_async_copy(krow, kext.at[pl.ds(1, cx), pl.ds(1, cy)], local_sem.at[1])
    inner_keys.start()
    own_meta = pltpu.make_async_copy(meta.at[me], meta_out.at[me], local_sem.at[2])
    own_meta.start()
    pl.semaphore_wait(barrier, groups + 1)

    def remote(src, dst, sems, index, to):
        return pltpu.make_async_remote_copy(
            src_ref=src, dst_ref=dst, send_sem=sems.at[(0, *index)], recv_sem=sems.at[(1, *index)],
            device_id=to, device_id_type=MESH,
        )

    ys = pl.ds(1, cy)
    xs = pl.ds(1, cx)
    faces = [
        (krow.at[cx - 1], kext.at[0, ys], up_x),
        (krow.at[0], kext.at[cx + 1, ys], down_x),
        (krow.at[:, cy - 1], kext.at[xs, 0], up_y),
        (krow.at[:, 0], kext.at[xs, cy + 1], down_y),
        (klast, kzlo, up_z),
        (kfirst, kzhi, down_z),
        (f.at[:, cy - 1], ext.at[xs, 0], up_y),
        (f.at[:, 0], ext.at[xs, cy + 1], down_y),
        (zlast, zlo, up_z),
        (zfirst, zhi, down_z),
    ]
    faces = [remote(src, dst, face_sem, (i,), to) for i, (src, dst, to) in enumerate(faces)]
    for copy in faces:
        copy.start()

    per = cy // xparts

    def x_copies(q):
        own, there = pl.ds(q * per, per), pl.ds(1 + q * per, per)
        return (
            remote(f.at[cx - 1, own], ext.at[0, there], x_sem, (0, q), up_x),
            remote(f.at[0, own], ext.at[cx + 1, there], x_sem, (1, q), down_x),
        )

    def x_start(q, carry):
        for copy in x_copies(q):
            copy.start()
        return carry

    lax.fori_loop(0, xparts, x_start, 0)

    def meta_copy(d, row):
        return remote(meta.at[(me + d) % groups], meta_out.at[row], meta_sem, (d,), peer(d))

    def meta_start(d, carry):
        meta_copy(d, me).start()
        return carry

    lax.fori_loop(1, groups, meta_start, 0)
    inner.wait()
    inner_keys.wait()
    own_meta.wait()
    for copy in faces:
        copy.wait()

    def one(n, carry):
        y, x = n // cx, n % cx
        i = x * cy + y
        outs = column(
            slots, sz,
            (ext[x, y + 1], ext[x + 2, y + 1]),
            (ext[x + 1, y], ext[x + 1, y + 2]),
            ext[x + 1, y + 1], (zlo[i], zhi[i]),
            (kext[x, y + 1], kext[x + 2, y + 1]),
            (kext[x + 1, y], kext[x + 1, y + 2]),
            kext[x + 1, y + 1], (kzlo[i], kzhi[i]),
            ids[i], coef[i], w_ref,
        )
        for t in range(4):
            pay[:, pl.ds(pl.multiple_of(i * sz, sz), sz), 128 * t : 128 * (t + 1)] = outs[t]
        return carry

    def part(q, carry):
        for copy in x_copies(q):
            copy.wait()
        lax.fori_loop(q * per * cx, (q + 1) * per * cx, one, 0)
        return carry

    lax.fori_loop(0, xparts, part, 0)

    cells = cx * cy * sz
    perm = jnp.where(lax.broadcasted_iota(jnp.int32, (cells, cells), 0) == pos[...], 1.0, 0.0).astype(jnp.bfloat16)
    step = slots // parts

    def move_copy(p, d, row):
        cut = pl.ds(p * step, step)
        return remote(sendb.at[(me + d) % groups, cut], out.at[row, cut], move_sem, (p, d), peer(d))

    def own_copy(p):
        cut = pl.ds(p * step, step)
        return pltpu.make_async_copy(sendb.at[me, cut], out.at[me, cut], local_sem.at[3 + p])

    def send(p, carry):
        for k in range(step):
            s = p * step + k
            rows = jnp.dot(perm, pay[s].astype(jnp.bfloat16), preferred_element_type=jnp.float32)
            for g in range(groups):
                sendb[g, s] = rows[g * cap : (g + 1) * cap].astype(jnp.bfloat16)

        def start(d, inner_carry):
            move_copy(p, d, me).start()
            return inner_carry

        lax.fori_loop(1, groups, start, 0)
        own_copy(p).start()
        return carry

    lax.fori_loop(0, parts, send, 0)

    def finish(d, carry):
        source = (me + groups - d) % groups
        copy = meta_copy(d, source)
        copy.wait_send()
        copy.wait_recv()
        return carry

    lax.fori_loop(1, groups, finish, 0)

    def finish_part(p, carry):
        own_copy(p).wait()

        def finish_one(d, inner_carry):
            copy = move_copy(p, d, (me + groups - d) % groups)
            copy.wait_send()
            copy.wait_recv()
            return inner_carry

        lax.fori_loop(1, groups, finish_one, 0)
        return carry

    lax.fori_loop(0, parts, finish_part, 0)


def on_device(distribution, block_ids, cell_counts, owner, restitution):
    cx, cy, sz, slots, vb = distribution.shape
    cells, rows, columns = cx * cy * sz, slots * sz, cx * cy
    groups = lax.axis_size("gx") * lax.axis_size("gz")
    cap = cells // groups
    live = jnp.arange(slots, dtype=jnp.int32) < cell_counts[..., None]
    listed = jnp.where(live, block_ids, -1).transpose(0, 1, 3, 2)
    f = distribution.transpose(0, 1, 3, 2, 4)
    pad = ((0, 0), (0, ZPAD - slots), (0, 0))
    zlast = jnp.pad(f[:, :, :, -1].reshape(columns, slots, vb), pad)
    zfirst = jnp.pad(f[:, :, :, 0].reshape(columns, slots, vb), pad)
    f = f.reshape(cx, cy, rows, vb)

    def lanes(keys):
        return jnp.pad(keys, ((0, 0),) * (keys.ndim - 1) + ((0, -keys.shape[-1] % 128),), constant_values=-9)

    krow = lanes((listed + 256 * jnp.arange(sz, dtype=jnp.int32)).reshape(cx, cy, 1, rows))
    klast = lanes(listed[..., -1].reshape(columns, 1, slots))
    kfirst = lanes((listed[..., 0] + 256 * (sz + 1)).reshape(columns, 1, slots))
    ids = listed.reshape(columns, rows, 1)
    coef = jnp.broadcast_to(restitution.astype(jnp.float32).reshape(columns, sz, 1), (columns, sz, 128))

    owners = owner.reshape(cells)
    order = jnp.arange(cells, dtype=jnp.int32)
    same = (owners[:, None] == owners[None, :]) & (order[:, None] < order[None, :])
    pos = owners * cap + jnp.sum(same.astype(jnp.int32), axis=0)

    meta = jnp.concatenate([block_ids.reshape(cells, slots), cell_counts.reshape(cells, 1)], axis=1)
    onehot = (order[:, None] == pos[None, :]).astype(jnp.bfloat16)
    meta = jnp.pad(meta.astype(jnp.bfloat16), ((0, 0), (0, 127 - slots)))
    meta = jnp.dot(onehot, meta, preferred_element_type=jnp.float32).astype(jnp.bfloat16)

    xparts = math.gcd(cy, XPARTS)
    parts = math.gcd(slots, PARTS)
    vmem, anywhere = pl.BlockSpec(memory_space=pltpu.VMEM), pl.BlockSpec(memory_space=pl.ANY)
    bf16, i32 = jnp.bfloat16, jnp.int32
    received, meta = pl.pallas_call(
        functools.partial(whole_kernel, (cx, cy, sz, slots, groups, cap, xparts, parts)),
        out_shape=(
            jax.ShapeDtypeStruct((groups, slots, cap, vb), bf16),
            jax.ShapeDtypeStruct((groups, cap, 128), bf16),
        ),
        in_specs=[anywhere] * 3 + [vmem] * 8,
        out_specs=(anywhere, anywhere),
        scratch_shapes=[
            pltpu.VMEM((cx + 2, cy + 2, rows, vb), bf16),
            pltpu.VMEM((columns, ZPAD, vb), bf16),
            pltpu.VMEM((columns, ZPAD, vb), bf16),
            pltpu.VMEM((cx + 2, cy + 2, 1, krow.shape[-1]), i32),
            pltpu.VMEM((columns, 1, 128), i32),
            pltpu.VMEM((columns, 1, 128), i32),
            pltpu.VMEM((slots, cells, vb), jnp.float32),
            pltpu.VMEM((groups, slots, cap, vb), bf16),
            pltpu.SemaphoreType.DMA((2, 2, xparts)),
            pltpu.SemaphoreType.DMA((2, 10)),
            pltpu.SemaphoreType.DMA((3 + parts,)),
            pltpu.SemaphoreType.DMA((2, parts, groups)),
            pltpu.SemaphoreType.DMA((2, groups)),
        ],
        compiler_params=pltpu.CompilerParams(
            collective_id=0, has_side_effects=True, vmem_limit_bytes=48 << 20
        ),
        name="transport_relax_move",
    )(f, zlast, zfirst, krow, klast, kfirst, meta.reshape(groups, cap, 128), ids, coef, weights(), pos.reshape(1, cells))
    moved = received.transpose(0, 2, 1, 3).reshape(1, cells, slots, vb)
    meta = meta.reshape(cells, 128)[:, : slots + 1].astype(i32)
    return moved, meta[:, :slots].reshape(1, cells, slots), meta[:, slots].reshape(1, cells)


def solution(mesh):
    placed = (
        P("gx", "gy", "gz", None, None),
        P("gx", "gy", "gz", None),
        P("gx", "gy", "gz"),
        P("gx", "gy", "gz"),
        P("gx", "gy", "gz"),
    )
    return jax.shard_map(
        on_device,
        mesh=mesh,
        in_specs=placed,
        out_specs=(
            P("gy", ("gx", "gz"), None, None),
            P("gy", ("gx", "gz"), None),
            P("gy", ("gx", "gz")),
        ),
        check_vma=False,
    )
```

```python
import functools
import math

import jax
import jax.numpy as jnp
import ml_dtypes
import numpy as np
from jax import lax
from jax.experimental import pallas as pl
from jax.experimental.pallas import tpu as pltpu
from jax.sharding import PartitionSpec as P

NV1 = 48
BLK = 8
EDGE = NV1 // BLK
STEP_COEFF = 0.6
IMPACT_KIND = 0.02
ZPAD = 16
XPARTS = 8
WINDOW = 3
PARTS = 4


def weights():
    j = np.arange(BLK**3)
    w = [c - (BLK - 1) / 2.0 for c in (j // (BLK * BLK), j // BLK % BLK, j % BLK)]
    cols = [np.ones(BLK**3), *w, w[0] * w[0] + w[1] * w[1] + w[2] * w[2]]
    return np.repeat(np.stack(cols, axis=1), 128, axis=1).astype(ml_dtypes.bfloat16)


def column(slots, sz, ext_x, ext_y, own, zrows, xkeys, ykeys, own_keys, zkeys, ids, coef, w_ref):
    rows = slots * sz
    shape = (rows, 128)
    listed = jnp.broadcast_to(ids, shape)
    live = listed >= 0
    z = lax.broadcasted_iota(jnp.int32, shape, 0) % sz
    bx = (listed * 1821) >> 16
    rem = listed - bx * (EDGE * EDGE)
    by = (rem * 10923) >> 16
    bz = rem - by * EDGE
    half = EDGE // 2

    dot = functools.partial(jnp.dot, preferred_element_type=jnp.float32)

    def pick(key, others, values):
        key = jnp.where(live, key, -5)[:, :1]
        total = None
        for other, value in zip(others, values):
            hit = jnp.where(key == other[:, : value.shape[0]], 1.0, 0.0).astype(jnp.bfloat16)
            got = dot(hit, value)
            total = got if total is None else total + got
        return total

    here = listed + 256 * z
    gx = pick(here + jnp.where(bx >= half, 0, 4096), (xkeys[0], xkeys[1] + 4096), ext_x)
    gy = pick(here + jnp.where(by >= half, 0, 4096), (ykeys[0], ykeys[1] + 4096), ext_y)
    zkey = listed + 256 * jnp.where(bz >= half, z, z + 2)
    gz = pick(zkey, (own_keys + 256, *zkeys), (own, *zrows))

    offset = (BLK - 1) / 2.0 - (NV1 - 1) / 2.0
    c = [b.astype(jnp.float32) * BLK + offset for b in (bx, by, bz)]
    lane = lax.broadcasted_iota(jnp.int32, (1, 128), 1)
    mid = (BLK - 1) / 2.0
    wx = [(lane // 64 + 2 * t).astype(jnp.float32) - mid for t in range(4)]
    wy = (lane // BLK % BLK).astype(jnp.float32) - mid
    wz = (lane % BLK).astype(jnp.float32) - mid
    vy, vz = jnp.abs(c[1] + wy), jnp.abs(c[2] + wz)
    lam = STEP_COEFF / (NV1 - 1)
    reads = []
    for t in range(4):
        cut = slice(128 * t, 128 * (t + 1))
        f = own[:, cut].astype(jnp.float32)
        flux = jnp.abs(c[0] + wx[t]) * (f - gx[:, cut]) + vy * (f - gy[:, cut]) + vz * (f - gz[:, cut])
        reads.append(jnp.where(live, f - lam * flux, 0.0).astype(jnp.bfloat16))
    sums = dot(reads[0], w_ref[0:128, :])
    for t in range(1, 4):
        sums = sums + dot(reads[t], w_ref[128 * t : 128 * (t + 1), :])
    s = [sums[:, 128 * k : 128 * (k + 1)] for k in range(5)]

    def per_cell(a):
        return jnp.sum(a.reshape(slots, sz, 128), axis=0)

    mass = per_cell(s[0])
    momentum = [per_cell(s[0] * c[k] + s[1 + k]) for k in range(3)]
    sq = c[0] * c[0] + c[1] * c[1] + c[2] * c[2]
    cross = c[0] * s[1] + c[1] * s[2] + c[2] * s[3]
    energy = per_cell(s[0] * sq + 2.0 * cross + s[4])
    u = [m / mass for m in momentum]
    temperature = (energy / mass - (u[0] * u[0] + u[1] * u[1] + u[2] * u[2])) / 3.0
    target = temperature * (1.0 + coef) * (1.0 + coef) / 4.0
    rate = 1.0 - jnp.exp(-IMPACT_KIND * (mass / BLK**3) * jnp.sqrt(temperature))
    area = 2.0 * math.pi * target
    scale = mass / (area * jnp.sqrt(area))
    inv = -0.5 / target

    cube = (slots, sz, 128)
    a = [c[k].reshape(cube) - u[k][None] for k in range(3)]
    oy, oz = a[1] + wy[None], a[2] + wz[None]
    q = oy * oy + oz * oz
    live3 = listed.reshape(cube) >= 0
    outs = []
    for t in range(4):
        ox = a[0] + wx[t][None]
        maxwellian = scale[None] * jnp.exp((ox * ox + q) * inv[None])
        r = reads[t].astype(jnp.float32).reshape(cube)
        outs.append(jnp.where(live3, r + rate[None] * (maxwellian - r), 0.0))
    return outs


MESH = pl.DeviceIdType.MESH


def whole_kernel(
    sizes, f, zlast, zfirst, krow, klast, kfirst, meta, ids, coef, w_ref, pos,
    out, meta_out,
    ext, zlo, zhi, kext, kzlo, kzhi, pay, sendb, x_sem, face_sem, local_sem, move_sem, meta_sem,
):
    cx, cy, sz, slots, groups, cap, xparts, parts = sizes
    gx, gy, gz = (lax.axis_index(a) for a in ("gx", "gy", "gz"))
    nx, ny, nz = (lax.axis_size(a) for a in ("gx", "gy", "gz"))
    me = gx * nz + gz
    up_x, down_x = ((gx + 1) % nx, gy, gz), ((gx + nx - 1) % nx, gy, gz)
    up_y, down_y = (gx, (gy + 1) % ny, gz), (gx, (gy + ny - 1) % ny, gz)
    up_z, down_z = (gx, gy, (gz + 1) % nz), (gx, gy, (gz + nz - 1) % nz)

    def peer(d):
        other = (me + d) % groups
        return other // nz, gy, other % nz

    barrier = pltpu.get_barrier_semaphore()
    pl.semaphore_signal(barrier, inc=1, device_id=up_y, device_id_type=MESH)
    pl.semaphore_signal(barrier, inc=1, device_id=down_y, device_id_type=MESH)

    def greet(d, carry):
        pl.semaphore_signal(barrier, inc=1, device_id=peer(d), device_id_type=MESH)
        return carry

    lax.fori_loop(1, groups, greet, 0)

    inner = pltpu.make_async_copy(f, ext.at[pl.ds(1, cx), pl.ds(1, cy)], local_sem.at[0])
    inner.start()
    inner_keys = pltpu.make_async_copy(krow, kext.at[pl.ds(1, cx), pl.ds(1, cy)], local_sem.at[1])
    inner_keys.start()
    own_meta = pltpu.make_async_copy(meta.at[me], meta_out.at[me], local_sem.at[2])
    own_meta.start()
    pl.semaphore_wait(barrier, groups + 1)

    def remote(src, dst, sems, index, to):
        return pltpu.make_async_remote_copy(
            src_ref=src, dst_ref=dst, send_sem=sems.at[(0, *index)], recv_sem=sems.at[(1, *index)],
            device_id=to, device_id_type=MESH,
        )

    ys = pl.ds(1, cy)
    xs = pl.ds(1, cx)
    faces = [
        (krow.at[cx - 1], kext.at[0, ys], up_x),
        (krow.at[0], kext.at[cx + 1, ys], down_x),
        (krow.at[:, cy - 1], kext.at[xs, 0], up_y),
        (krow.at[:, 0], kext.at[xs, cy + 1], down_y),
        (klast, kzlo, up_z),
        (kfirst, kzhi, down_z),
        (f.at[:, cy - 1], ext.at[xs, 0], up_y),
        (f.at[:, 0], ext.at[xs, cy + 1], down_y),
        (zlast, zlo, up_z),
        (zfirst, zhi, down_z),
    ]
    faces = [remote(src, dst, face_sem, (i,), to) for i, (src, dst, to) in enumerate(faces)]
    for copy in faces:
        copy.start()

    per = cy // xparts

    def x_copies(q):
        own, there = pl.ds(q * per, per), pl.ds(1 + q * per, per)
        return (
            remote(f.at[cx - 1, own], ext.at[0, there], x_sem, (0, q), up_x),
            remote(f.at[0, own], ext.at[cx + 1, there], x_sem, (1, q), down_x),
        )

    def x_start(q, carry):
        for copy in x_copies(q):
            copy.start()
        return carry

    lax.fori_loop(0, min(WINDOW, xparts), x_start, 0)

    def meta_copy(d, row):
        return remote(meta.at[(me + d) % groups], meta_out.at[row], meta_sem, (d,), peer(d))

    def meta_start(d, carry):
        meta_copy(d, me).start()
        return carry

    lax.fori_loop(1, groups, meta_start, 0)
    inner.wait()
    inner_keys.wait()
    own_meta.wait()
    for copy in faces:
        copy.wait()

    def one(n, carry):
        y, x = n // cx, n % cx
        i = x * cy + y
        outs = column(
            slots, sz,
            (ext[x, y + 1], ext[x + 2, y + 1]),
            (ext[x + 1, y], ext[x + 1, y + 2]),
            ext[x + 1, y + 1], (zlo[i], zhi[i]),
            (kext[x, y + 1], kext[x + 2, y + 1]),
            (kext[x + 1, y], kext[x + 1, y + 2]),
            kext[x + 1, y + 1], (kzlo[i], kzhi[i]),
            ids[i], coef[i], w_ref,
        )
        for t in range(4):
            pay[:, pl.ds(pl.multiple_of(i * sz, sz), sz), 128 * t : 128 * (t + 1)] = outs[t]
        return carry

    def part(q, carry):
        for copy in x_copies(q):
            copy.wait()

        @pl.when(q + WINDOW < xparts)
        def _():
            x_start(q + WINDOW, 0)

        lax.fori_loop(q * per * cx, (q + 1) * per * cx, one, 0)
        return carry

    lax.fori_loop(0, xparts, part, 0)

    cells = cx * cy * sz
    perm = jnp.where(lax.broadcasted_iota(jnp.int32, (cells, cells), 0) == pos[...], 1.0, 0.0).astype(jnp.bfloat16)
    step = slots // parts

    def move_copy(p, d, row):
        cut = pl.ds(p * step, step)
        return remote(sendb.at[(me + d) % groups, cut], out.at[row, cut], move_sem, (p, d), peer(d))

    def own_copy(p):
        cut = pl.ds(p * step, step)
        return pltpu.make_async_copy(sendb.at[me, cut], out.at[me, cut], local_sem.at[3 + p])

    def send(p, carry):
        for k in range(step):
            s = p * step + k
            rows = jnp.dot(perm, pay[s].astype(jnp.bfloat16), preferred_element_type=jnp.float32)
            for g in range(groups):
                sendb[g, s] = rows[g * cap : (g + 1) * cap].astype(jnp.bfloat16)

        def start(d, inner_carry):
            move_copy(p, d, me).start()
            return inner_carry

        lax.fori_loop(1, groups, start, 0)
        own_copy(p).start()
        return carry

    lax.fori_loop(0, parts, send, 0)

    def finish(d, carry):
        source = (me + groups - d) % groups
        copy = meta_copy(d, source)
        copy.wait_send()
        copy.wait_recv()
        return carry

    lax.fori_loop(1, groups, finish, 0)

    def finish_part(p, carry):
        own_copy(p).wait()

        def finish_one(d, inner_carry):
            copy = move_copy(p, d, (me + groups - d) % groups)
            copy.wait_send()
            copy.wait_recv()
            return inner_carry

        lax.fori_loop(1, groups, finish_one, 0)
        return carry

    lax.fori_loop(0, parts, finish_part, 0)


def on_device(distribution, block_ids, cell_counts, owner, restitution):
    cx, cy, sz, slots, vb = distribution.shape
    cells, rows, columns = cx * cy * sz, slots * sz, cx * cy
    groups = lax.axis_size("gx") * lax.axis_size("gz")
    cap = cells // groups
    live = jnp.arange(slots, dtype=jnp.int32) < cell_counts[..., None]
    listed = jnp.where(live, block_ids, -1).transpose(0, 1, 3, 2)
    f = distribution.transpose(0, 1, 3, 2, 4)
    pad = ((0, 0), (0, ZPAD - slots), (0, 0))
    zlast = jnp.pad(f[:, :, :, -1].reshape(columns, slots, vb), pad)
    zfirst = jnp.pad(f[:, :, :, 0].reshape(columns, slots, vb), pad)
    f = f.reshape(cx, cy, rows, vb)

    def lanes(keys):
        return jnp.pad(keys, ((0, 0),) * (keys.ndim - 1) + ((0, -keys.shape[-1] % 128),), constant_values=-9)

    krow = lanes((listed + 256 * jnp.arange(sz, dtype=jnp.int32)).reshape(cx, cy, 1, rows))
    klast = lanes(listed[..., -1].reshape(columns, 1, slots))
    kfirst = lanes((listed[..., 0] + 256 * (sz + 1)).reshape(columns, 1, slots))
    ids = listed.reshape(columns, rows, 1)
    coef = jnp.broadcast_to(restitution.astype(jnp.float32).reshape(columns, sz, 1), (columns, sz, 128))

    owners = owner.reshape(cells)
    order = jnp.arange(cells, dtype=jnp.int32)
    same = (owners[:, None] == owners[None, :]) & (order[:, None] < order[None, :])
    pos = owners * cap + jnp.sum(same.astype(jnp.int32), axis=0)

    meta = jnp.concatenate([block_ids.reshape(cells, slots), cell_counts.reshape(cells, 1)], axis=1)
    onehot = (order[:, None] == pos[None, :]).astype(jnp.bfloat16)
    meta = jnp.pad(meta.astype(jnp.bfloat16), ((0, 0), (0, 127 - slots)))
    meta = jnp.dot(onehot, meta, preferred_element_type=jnp.float32).astype(jnp.bfloat16)

    xparts = math.gcd(cy, XPARTS)
    parts = math.gcd(slots, PARTS)
    vmem, anywhere = pl.BlockSpec(memory_space=pltpu.VMEM), pl.BlockSpec(memory_space=pl.ANY)
    bf16, i32 = jnp.bfloat16, jnp.int32
    received, meta = pl.pallas_call(
        functools.partial(whole_kernel, (cx, cy, sz, slots, groups, cap, xparts, parts)),
        out_shape=(
            jax.ShapeDtypeStruct((groups, slots, cap, vb), bf16),
            jax.ShapeDtypeStruct((groups, cap, 128), bf16),
        ),
        in_specs=[anywhere] * 3 + [vmem] * 8,
        out_specs=(anywhere, anywhere),
        scratch_shapes=[
            pltpu.VMEM((cx + 2, cy + 2, rows, vb), bf16),
            pltpu.VMEM((columns, ZPAD, vb), bf16),
            pltpu.VMEM((columns, ZPAD, vb), bf16),
            pltpu.VMEM((cx + 2, cy + 2, 1, krow.shape[-1]), i32),
            pltpu.VMEM((columns, 1, 128), i32),
            pltpu.VMEM((columns, 1, 128), i32),
            pltpu.VMEM((slots, cells, vb), jnp.float32),
            pltpu.VMEM((groups, slots, cap, vb), bf16),
            pltpu.SemaphoreType.DMA((2, 2, xparts)),
            pltpu.SemaphoreType.DMA((2, 10)),
            pltpu.SemaphoreType.DMA((3 + parts,)),
            pltpu.SemaphoreType.DMA((2, parts, groups)),
            pltpu.SemaphoreType.DMA((2, groups)),
        ],
        compiler_params=pltpu.CompilerParams(
            collective_id=0, has_side_effects=True, vmem_limit_bytes=48 << 20
        ),
        name="transport_relax_move",
    )(f, zlast, zfirst, krow, klast, kfirst, meta.reshape(groups, cap, 128), ids, coef, jnp.asarray(weights()), pos.reshape(1, cells))
    moved = received.transpose(0, 2, 1, 3).reshape(1, cells, slots, vb)
    meta = meta.reshape(cells, 128)[:, : slots + 1].astype(i32)
    return moved, meta[:, :slots].reshape(1, cells, slots), meta[:, slots].reshape(1, cells)


def solution(mesh):
    placed = (
        P("gx", "gy", "gz", None, None),
        P("gx", "gy", "gz", None),
        P("gx", "gy", "gz"),
        P("gx", "gy", "gz"),
        P("gx", "gy", "gz"),
    )
    return jax.shard_map(
        on_device,
        mesh=mesh,
        in_specs=placed,
        out_specs=(
            P("gy", ("gx", "gz"), None, None),
            P("gy", ("gx", "gz"), None),
            P("gy", ("gx", "gz")),
        ),
        check_vma=False,
    )
```
